1024 devices in a mesh: row: 16 (over y, core), col: 64 (over x, z).
Axes of the slice: x: 4, y: 8, z: 16, core: 2. Of those that a mesh axis runs over, the one named last changes fastest.
Arguments:
- obj_slices: float32 [2, 2, 2048, 8192], P(None, None, 'row', 'col'), may hold values from -5 to 5
- probe_wave: float32 [2, 128, 128], replicated, may hold values from -5 to 5
- prop_phase: float32 [128, 128], replicated, may hold values from -3.140625 to 3.140625
- measured: float32 [16, 64, 2, 128, 128], P('row', 'col'), may hold values from 0 to 2
- positions: int32 [16, 64, 2, 2], P('row', 'col'), may hold values from 0 to 8064, as said below
- counts: int32 [16, 64], P('row', 'col'), may hold values from 0 to 2, as said below
Outputs:
- gradient: float32 [2, 2, 2048, 8192], P(None, None, 'row', 'col')
The draws below stay inside these ranges and needn't reach their ends.
Inputs may be any that keep to these rules, and one draw needn't show every extreme that they name: `positions`: for the device at mesh row r and column c, each window starts at row min(max(r * 128 - 64 + u, 0), 1920) and column min(max(c * 128 - 64 + v, 0), 8064) for some 0 <= u < 128, 0 <= v < 128; dimension 2 holds the row, then the column. `counts`: live slots are the first ones of a device. The devices at mesh columns 2 * i and 2 * i + 1 of one mesh row hold at most 2 live slots together, and in every draw some device holds 2.
All inputs are finite; a program needn't handle non-finite values.
Results may differ from the reference program's by a relative error of at most 0.0003.
Values sent between devices are 32-bit elements; how exact they have to be, the bound alone decides.
No kernel may reach another device: no remote copies, remote signals or barrier semaphores. Data moves between devices by JAX's collectives and lax.ppermute only.
A program may use at most 32 MiB of HBM per device.

```python
import jax
import jax.numpy as jnp
from jax import lax

P_SIZE = 128
S = 2
K = 2
TR = 128
TC = 128
RIM = 64
NR = 2048
NC = 8192
SCAN_R = 16
SCAN_C = 64


def draw_positions(key, part):
    key = jax.random.fold_in(key, 11)
    key_rows, key_cols = jax.random.split(key)
    offset_rows = jax.random.randint(key_rows, (SCAN_R, SCAN_C, K), 0, TR)
    offset_cols = jax.random.randint(key_cols, (SCAN_R, SCAN_C, K), 0, TC)
    base_rows = jnp.arange(SCAN_R, dtype=jnp.int32)[:, None, None] * TR - RIM
    base_cols = jnp.arange(SCAN_C, dtype=jnp.int32)[None, :, None] * TC - RIM
    start_rows = jnp.clip(base_rows + offset_rows, 0, NR - P_SIZE)
    start_cols = jnp.clip(base_cols + offset_cols, 0, NC - P_SIZE)
    return jnp.stack([start_rows, start_cols], axis=2).astype(jnp.int32)


def draw_counts(key, part):
    key = jax.random.fold_in(key, 23)
    key_first, key_second, key_flip, key_pick = jax.random.split(key, 4)
    pair_cols = SCAN_C // 2
    first_load = jax.random.randint(key_first, (SCAN_R, pair_cols), 0, K + 1)
    second_load = jax.random.randint(key_second, (SCAN_R, pair_cols), 0, K - first_load + 1)
    chosen = jax.random.randint(key_pick, (), 0, SCAN_R * pair_cols)
    forced = jnp.arange(SCAN_R * pair_cols, dtype=jnp.int32).reshape(SCAN_R, pair_cols) == chosen
    first_load = jnp.where(forced, K, first_load)
    second_load = jnp.where(forced, 0, second_load)
    flipped = jax.random.randint(key_flip, (SCAN_R, pair_cols), 0, 2) == 1
    left_load = jnp.where(flipped, second_load, first_load)
    right_load = jnp.where(flipped, first_load, second_load)
    return jnp.stack([left_load, right_load], axis=2).reshape(SCAN_R, SCAN_C).astype(jnp.int32)


def block_scale(rng, extent, cuts, low, top_value):
    def one(axis_at, shards_of):
        draws = jax.random.uniform(jax.random.fold_in(jax.random.fold_in(rng, 6), axis_at), (shards_of,), jnp.float32, low / len(cuts), top_value / len(cuts))
        return jnp.repeat(jnp.exp(draws), extent[axis_at] // shards_of).reshape((-1,) + (1,) * (len(extent) - axis_at - 1))

    loudness = one(*cuts[0])
    for cut in cuts[1:]:
        loudness = loudness * one(*cut)
    return loudness


def noise(own_key, extent, spread, limit, cuts=(), kind=jnp.bfloat16):
    array = jax.random.normal(own_key, extent, jnp.float32) * spread
    if len(cuts) > 0:
        array = block_scale(own_key, extent, cuts, -0.22, 0.18) * array
    return jnp.clip(array, min=-limit, max=limit).astype(kind)


def setup_inputs(seed: int = 0) -> dict:
    key_of = jax.random.split(jax.random.key(seed), 7)
    return {
        "obj_slices": noise(key_of[0], (2, S, NR, NC), 0.7, 5.0, ((2, 16), (3, 64)), jnp.float32),
        "probe_wave": noise(key_of[1], (2, P_SIZE, P_SIZE), 0.7, 5.0, (), jnp.float32),
        "prop_phase": jnp.clip(jax.random.uniform(key_of[2], (P_SIZE, P_SIZE), jnp.float32, -3.140625, 3.140625), -3.140625, 3.140625),
        "measured": jnp.clip(2.0 * jax.random.uniform(key_of[3], (SCAN_R, SCAN_C, K, P_SIZE, P_SIZE), jnp.float32) ** block_scale(key_of[3], (SCAN_R, SCAN_C, K, P_SIZE, P_SIZE), ((0, 16), (1, 64)), -0.2, 0.2), 0.0, 2.0),
        "positions": draw_positions(jax.random.fold_in(key_of[6], 71), 0),
        "counts": draw_counts(jax.random.fold_in(key_of[6], 71), 0),
    }


def slot_loss(patch, probe_wave, kernel, target):
    wave_field = probe_wave[0] + 1j * probe_wave[1]
    slab_count = patch.shape[1]
    for slab_index in range(slab_count):
        wave_field = (patch[0, slab_index] + 1j * patch[1, slab_index]) * wave_field
        if slab_index + 1 < slab_count:
            spectrum = kernel * jnp.fft.fft2(wave_field, norm='ortho')
            wave_field = jnp.fft.ifft2(spectrum, norm='ortho')
    far_field = jnp.fft.fft2(wave_field, norm='ortho')
    misfit = jnp.real(far_field) ** 2 + jnp.imag(far_field) ** 2 - target
    return 0.25 * jnp.sum(misfit * misfit)

def reference(obj_slices, probe_wave, prop_phase, measured, positions, counts):
    kernel = jnp.cos(prop_phase) + 1j * jnp.sin(prop_phase)
    grad_slot = jax.grad(slot_loss)
    sequence_length = probe_wave.shape[1]
    slab_count = obj_slices.shape[1]
    slot_count = positions.shape[3]
    flattened_probe_positions = positions.reshape(-1, 2, slot_count)
    flattened_measurements = measured.reshape(-1, slot_count, sequence_length, sequence_length)
    slot_ids = jnp.arange(slot_count, dtype=jnp.int32)
    slot_active_mask = (slot_ids[None, :] < counts.reshape(-1, 1).astype(jnp.int32)).astype(jnp.float32)
    zero_index = jnp.zeros((), jnp.int32)

    def single_processor(running, element):
        starts, targets, live_row = element

        def cut_patch(start_y, start_x):
            return lax.dynamic_slice(obj_slices, (zero_index, zero_index, start_y.astype(jnp.int32), start_x.astype(jnp.int32)), (2, slab_count, sequence_length, sequence_length))
        patches = jax.vmap(cut_patch)(starts[0], starts[1])
        slot_grads = jax.vmap(grad_slot, in_axes=(0, None, None, 0))(patches, probe_wave, kernel, targets)
        slot_grads = slot_grads * live_row.astype(slot_grads.dtype)[:, None, None, None, None]

        def add_patch(slot_index, buffer):
            anchor = (zero_index, zero_index, starts[0, slot_index].astype(jnp.int32), starts[1, slot_index].astype(jnp.int32))
            current = lax.dynamic_slice(buffer, anchor, (2, slab_count, sequence_length, sequence_length))
            return lax.dynamic_update_slice(buffer, current + slot_grads[slot_index].astype(buffer.dtype), anchor)
        running = lax.fori_loop(0, slot_count, add_patch, running)
        return (running, None)
    starting_value = jnp.zeros(obj_slices.shape, jnp.float32)
    gradient, unused_item = lax.scan(single_processor, starting_value, (flattened_probe_positions, flattened_measurements, slot_active_mask))
    return gradient
```

```python
import math

import jax
import jax.numpy as jnp
import numpy as np
from jax import lax
from jax.experimental import pallas as pl
from jax.experimental.pallas import tpu as pltpu
from jax.sharding import PartitionSpec as P

N = 128
H = N // 2
F32 = jnp.float32
BF16 = jnp.bfloat16
VMEM = pl.BlockSpec(memory_space=pltpu.VMEM)
SMEM = pl.BlockSpec(memory_space=pltpu.SMEM)


def dft_tables():
    index = np.arange(N)
    angle = (index[:, None] * index[None, :] % N) * (-2.0 * math.pi / N)
    re, im = np.cos(angle) / math.sqrt(N), np.sin(angle) / math.sqrt(N)
    table = np.block([[re, im], [-im, re]]).astype(np.float32)
    out = []
    for one in (table, table.T):
        high = one.astype(jnp.bfloat16)
        out += [high, (one - high.astype(np.float32)).astype(jnp.bfloat16)]
    return np.stack(out)


def swap_half(value):
    return pltpu.roll(value, H, value.ndim - 1)


def low_lanes(shape):
    return lax.broadcasted_iota(jnp.int32, shape, len(shape) - 1) < H


def pack_left(top, bottom, low):
    return jnp.where(low, top, bottom)


def pack_right(top, bottom, low):
    return jnp.where(low, bottom, top)


def pack_kernel(obj_ref, left_ref, right_ref):
    low = low_lanes((H, N))
    for i in range(2):
        for j in range(2):
            top = obj_ref[i, j, :H, :]
            bottom = swap_half(obj_ref[i, j, H:, :])
            left_ref[i, j] = pack_left(top, bottom, low)
            right_ref[i, j] = pack_right(top, bottom, low)


def rows_kernel(obj_ref, from_left_ref, from_right_ref, up_ref, down_ref):
    low = low_lanes((H, N))
    for i in range(2):
        for j in range(2):
            first, second = from_right_ref[i, j], from_left_ref[i, j]
            up_ref[i, j, :, :N] = obj_ref[i, j, :H, :]
            up_ref[i, j, :, N:] = jnp.where(low, first, second)
            down_ref[i, j, :, :N] = obj_ref[i, j, H:, :]
            down_ref[i, j, :, N:] = swap_half(jnp.where(low, second, first))


def split(value):
    high = value.astype(BF16)
    return high, (value - high.astype(F32)).astype(BF16)


def dot(a, b):
    return jnp.dot(a, b, preferred_element_type=F32)


def from_right(value, high, low):
    v_high, v_low = split(value)
    return dot(v_high, high) + (dot(v_low, high) + dot(v_high, low))


def from_left(high, low, value):
    v_high, v_low = split(value)
    return dot(high, v_high) + (dot(high, v_low) + dot(low, v_high))


def regroup(value):
    return jnp.concatenate(
        [
            jnp.concatenate([value[:N, :N], value[N:, :N]], axis=1),
            jnp.concatenate([value[:N, N:], value[N:, N:]], axis=1),
        ],
        axis=0,
    )


def main_kernel(
    scal_ref,
    up_ref,
    down_ref,
    above_ref,
    below_ref,
    probe_ref,
    kernel_ref,
    measured_ref,
    table_ref,
    mid_ref,
    high_ref,
    low_ref,
    ext,
    acc,
):
    for i in range(2):
        for j in range(2):
            k = 2 * i + j
            ext[k, 0:H, :] = above_ref[i, j]
            ext[k, H : 2 * H, :] = up_ref[i, j]
            ext[k, 2 * H : 3 * H, :] = down_ref[i, j]
            ext[k, 3 * H :, :] = below_ref[i, j]
    lane = lax.broadcasted_iota(jnp.int32, (N + 8, N), 1)
    live = scal_ref[4]
    sub = lax.broadcasted_iota(jnp.int32, (N // 8, 8, N), 1)
    rows, turns, masks = [], [], []
    for slot in range(2):
        row, column = scal_ref[2 * slot], scal_ref[2 * slot + 1]
        turn = jnp.where(column < H, column + H, column - H)
        masks.append((lane >= turn) != (column < H))
        rows.append(row)
        turns.append(turn)

    def align(slot):
        odd = lax.rem(rows[slot], 8)
        return pl.multiple_of(rows[slot] - odd, 8), odd

    def cut(k, slot):
        back = jnp.where(turns[slot] == 0, 0, N - turns[slot])
        start, odd = align(slot)
        first = pltpu.roll(ext[k, pl.ds(start, N + 8), :N], back, 1)
        second = pltpu.roll(ext[k, pl.ds(start, N + 8), N:], back, 1)
        inside = (lane < N - turns[slot]) != (scal_ref[2 * slot + 1] < H)
        value = jnp.where(inside, first, second).reshape(N // 8 + 1, 8, N)
        value = pltpu.roll(value, jnp.where(odd == 0, 0, 8 - odd), 1)
        return jnp.where(sub < 8 - odd, value[:-1], value[1:]).reshape(N, N)

    def both(j):
        re = jnp.concatenate([cut(j, 0), cut(j, 1)], axis=0)
        im = jnp.concatenate([cut(2 + j, 0), cut(2 + j, 1)], axis=0)
        return re, im

    def twice(value):
        return jnp.concatenate([value, value], axis=0)

    f_high, f_low, b_high, b_low = (table_ref[i] for i in range(4))

    def join(re, im):
        return jnp.concatenate([re, im], axis=1)

    def forward(re, im):
        half = from_right(join(re, im), f_high, f_low)
        out = from_left(b_high, b_low, regroup(half))
        return out[:N], out[N:]

    def backward(re, im):
        half = from_left(f_high, f_low, jnp.concatenate([re, im], axis=0))
        out = from_right(regroup(half), b_high, b_low)
        return out[:, :N], out[:, N:]

    probe_re, probe_im = twice(probe_ref[0]), twice(probe_ref[1])
    k_re = jnp.concatenate([kernel_ref[0], kernel_ref[0]], axis=1)
    k_im = jnp.concatenate([kernel_ref[1], kernel_ref[1]], axis=1)
    t_re, t_im = both(0)
    w_re = t_re * probe_re - t_im * probe_im
    w_im = t_re * probe_im + t_im * probe_re
    s_re, s_im = forward(w_re, w_im)
    s_re, s_im = k_re * s_re - k_im * s_im, k_re * s_im + k_im * s_re
    p_re, p_im = backward(s_re, s_im)
    t_re, t_im = both(1)
    w_re = t_re * p_re - t_im * p_im
    w_im = t_re * p_im + t_im * p_re
    far_re, far_im = forward(w_re, w_im)
    target = jnp.concatenate([measured_ref[0], measured_ref[1]], axis=1)
    misfit = far_re * far_re + far_im * far_im - target
    g_re, g_im = backward(misfit * far_re, misfit * far_im)

    def add(k, value):
        for slot in range(2):
            turned = pltpu.roll(value[slot * N : (slot + 1) * N], turns[slot], 1)
            turned = jnp.where(slot < live, turned, 0.0)
            start, odd = align(slot)
            turned = pltpu.roll(turned.reshape(N // 8, 8, N), odd, 1)
            none = jnp.zeros((1, 8, N), F32)
            turned = jnp.concatenate(
                [
                    jnp.where(sub[:1] < odd, none, turned[:1]),
                    jnp.where(sub[1:] < odd, turned[:-1], turned[1:]),
                    jnp.where(sub[:1] < odd, turned[-1:], none),
                ],
                axis=0,
            ).reshape(N + 8, N)
            where = pl.ds(start, N + 8)
            acc[k, where, :N] += jnp.where(masks[slot], turned, 0.0)
            acc[k, where, N:] += jnp.where(masks[slot], 0.0, turned)

    acc[...] = jnp.zeros_like(acc)
    add(1, p_re * g_re + p_im * g_im)
    add(3, p_re * g_im - p_im * g_re)
    g_re, g_im = t_re * g_re + t_im * g_im, t_re * g_im - t_im * g_re
    s_re, s_im = forward(g_re, g_im)
    s_re, s_im = k_re * s_re + k_im * s_im, k_re * s_im - k_im * s_re
    g_re, g_im = backward(s_re, s_im)
    add(0, probe_re * g_re + probe_im * g_im)
    add(2, probe_re * g_im - probe_im * g_re)
    for i in range(2):
        for j in range(2):
            k = 2 * i + j
            low_ref[i, j] = acc[k, 0:H, :]
            mid_ref[i, j] = acc[k, H : 3 * H, :]
            high_ref[i, j] = acc[k, 3 * H :, :]


def fold_rows_kernel(mid_ref, above_ref, below_ref, own_ref, left_ref, right_ref):
    low = low_lanes((H, N))
    for i in range(2):
        for j in range(2):
            top = mid_ref[i, j, :H, :] + above_ref[i, j]
            bottom = mid_ref[i, j, H:, :] + below_ref[i, j]
            own_ref[i, j, :H, :] = top[:, :N]
            own_ref[i, j, H:, :] = bottom[:, :N]
            top, bottom = top[:, N:], swap_half(bottom[:, N:])
            right_ref[i, j] = pack_left(top, bottom, low)
            left_ref[i, j] = pack_right(top, bottom, low)


def fold_columns_kernel(own_ref, from_left_ref, from_right_ref, out_ref):
    low = low_lanes((H, N))
    for i in range(2):
        for j in range(2):
            first, second = from_left_ref[i, j], from_right_ref[i, j]
            out_ref[i, j, :H, :] = own_ref[i, j, :H, :] + jnp.where(low, first, second)
            out_ref[i, j, H:, :] = own_ref[i, j, H:, :] + swap_half(
                jnp.where(low, second, first)
            )


def call(body, shapes, *operands, specs=None, scratch=(), name=None, flops=0):
    outs = [jax.ShapeDtypeStruct(shape, F32) for shape in shapes]
    size = 4 * sum(math.prod(s) for s in shapes) + sum(4 * o.size for o in operands)
    return pl.pallas_call(
        body,
        out_shape=outs,
        in_specs=specs or [VMEM] * len(operands),
        out_specs=[VMEM] * len(outs),
        scratch_shapes=list(scratch),
        compiler_params=pltpu.CompilerParams(vmem_limit_bytes=32 * 2**20),
        cost_estimate=pl.CostEstimate(flops=flops, bytes_accessed=size, transcendentals=0),
        name=name,
    )(*operands)


def to_next(value, axis):
    count = lax.axis_size(axis)
    return lax.ppermute(value, axis, [(i, i + 1) for i in range(count - 1)])


def to_previous(value, axis):
    count = lax.axis_size(axis)
    return lax.ppermute(value, axis, [(i + 1, i) for i in range(count - 1)])


def per_device(obj_slices, probe_wave, prop_phase, measured, positions, counts):
    packed = (2, 2, H, N)
    strip = (2, 2, H, 2 * N)
    tile = (2, 2, N, N)
    local_y = positions[0, 0, 0] - lax.axis_index("row") * N + H
    local_x = positions[0, 0, 1] - lax.axis_index("col") * N + H
    scalars = jnp.stack([local_y[0], local_x[0], local_y[1], local_x[1], counts[0, 0]])
    kernel = jnp.stack([jnp.cos(prop_phase), jnp.sin(prop_phase)])
    tables = jnp.asarray(dft_tables())

    left, right = call(pack_kernel, [packed] * 2, obj_slices, name="pack_columns")
    from_left, from_right = to_next(right, "col"), to_previous(left, "col")
    up, down = call(
        rows_kernel, [strip] * 2, obj_slices, from_left, from_right, name="pack_rows"
    )
    above, below = to_next(down, "row"), to_previous(up, "row")
    mid, high, low = call(
        main_kernel,
        [(2, 2, N, 2 * N), strip, strip],
        scalars,
        up,
        down,
        above,
        below,
        probe_wave,
        kernel,
        measured[0, 0],
        tables,
        specs=[SMEM] + [VMEM] * 8,
        scratch=[pltpu.VMEM((4, 2 * N, 2 * N), F32), pltpu.VMEM((4, 2 * N, 2 * N), F32)],
        name="window_gradients",
        flops=36 * 2 * 256**3,
    )
    above, below = to_next(high, "row"), to_previous(low, "row")
    own, left, right = call(
        fold_rows_kernel, [tile, packed, packed], mid, above, below, name="fold_rows"
    )
    from_left, from_right = to_next(right, "col"), to_previous(left, "col")
    (out,) = call(
        fold_columns_kernel, [tile], own, from_left, from_right, name="fold_columns"
    )
    return out


def solution(mesh):
    placed = (
        P(None, None, "row", "col"),
        P(),
        P(),
        P("row", "col", None, None, None),
        P("row", "col", None, None),
        P("row", "col"),
    )
    return jax.shard_map(
        per_device,
        mesh=mesh,
        in_specs=placed,
        out_specs=P(None, None, "row", "col"),
        check_vma=False,
    )
```

```python
import math

import jax
import jax.numpy as jnp
import numpy as np
from jax import lax
from jax.experimental import pallas as pl
from jax.experimental.pallas import tpu as pltpu
from jax.sharding import PartitionSpec as P

N = 128
H = N // 2
F32 = jnp.float32
BF16 = jnp.bfloat16
VMEM = pl.BlockSpec(memory_space=pltpu.VMEM)
SMEM = pl.BlockSpec(memory_space=pltpu.SMEM)


def dft_tables():
    index = np.arange(N)
    angle = (index[:, None] * index[None, :] % N) * (-2.0 * math.pi / N)
    re, im = np.cos(angle) / math.sqrt(N), np.sin(angle) / math.sqrt(N)
    table = np.block([[re, im], [-im, re]]).astype(np.float32)
    out = []
    for one in (table, table.T):
        high = one.astype(jnp.bfloat16)
        out += [high, (one - high.astype(np.float32)).astype(jnp.bfloat16)]
    return np.stack(out)


def swap_half(value):
    return pltpu.roll(value, H, value.ndim - 1)


def low_lanes(shape):
    return lax.broadcasted_iota(jnp.int32, shape, len(shape) - 1) < H


def parity_of(axis):
    return lax.rem(lax.axis_index(axis), 2)


def pack_columns(top, bottom, parity):
    bottom = swap_half(bottom)
    low = low_lanes((H, N)) != (parity == 1)
    return jnp.where(low, bottom, top), jnp.where(low, top, bottom)


def unpack_columns(even, odd, parity):
    low = low_lanes((H, N)) != (parity == 1)
    return jnp.where(low, even, odd), swap_half(jnp.where(low, odd, even))


def pack_kernel(obj_ref, even_ref, odd_ref):
    parity = parity_of("col")
    for i in range(2):
        for j in range(2):
            even_ref[i, j], odd_ref[i, j] = pack_columns(
                obj_ref[i, j, :H, :], obj_ref[i, j, H:, :], parity
            )


def rows_kernel(obj_ref, even_ref, odd_ref, row_even_ref, row_odd_ref):
    parity = parity_of("col")
    row_parity = parity_of("row")
    for i in range(2):
        for j in range(2):
            top, bottom = unpack_columns(even_ref[1 - parity, i, j], odd_ref[i, j], parity)
            top = jnp.concatenate([obj_ref[i, j, :H, :], top], axis=1)
            bottom = jnp.concatenate([obj_ref[i, j, H:, :], bottom], axis=1)
            row_even_ref[i, j] = jnp.where(row_parity == 0, bottom, top)
            row_odd_ref[i, j] = jnp.where(row_parity == 0, top, bottom)


def split(value):
    high = value.astype(BF16)
    return high, (value - high.astype(F32)).astype(BF16)


def dot(a, b):
    return jnp.dot(a, b, preferred_element_type=F32)


def from_right(value, high, low):
    v_high, v_low = split(value)
    return dot(v_high, high) + (dot(v_low, high) + dot(v_high, low))


def from_left(high, low, value):
    v_high, v_low = split(value)
    return dot(high, v_high) + (dot(high, v_low) + dot(low, v_high))


def regroup(value):
    return jnp.concatenate(
        [
            jnp.concatenate([value[:N, :N], value[N:, :N]], axis=1),
            jnp.concatenate([value[:N, N:], value[N:, N:]], axis=1),
        ],
        axis=0,
    )


def main_kernel(
    positions_ref,
    counts_ref,
    own_even_ref,
    own_odd_ref,
    even_ref,
    odd_ref,
    probe_ref,
    kernel_ref,
    measured_ref,
    table_ref,
    mid_ref,
    to_even_ref,
    to_odd_ref,
    ext,
    acc,
):
    row_parity = parity_of("row")

    def strip(number):
        return pl.ds(pl.multiple_of(jnp.where(row_parity == 0, number, 3 - number) * H, H), H)

    for i in range(2):
        for j in range(2):
            k = 2 * i + j
            ext[k, strip(0), :] = odd_ref[i, j]
            ext[k, strip(1), :] = own_odd_ref[i, j]
            ext[k, strip(2), :] = own_even_ref[i, j]
            ext[k, strip(3), :] = even_ref[1 - row_parity, i, j]
    lane = lax.broadcasted_iota(jnp.int32, (N + 8, N), 1)
    live = counts_ref[0, 0]
    sub = lax.broadcasted_iota(jnp.int32, (N // 8, 8, N), 1)
    rows, turns, masks, wraps = [], [], [], []
    for slot in range(2):
        row = positions_ref[0, 0, 0, slot] - lax.axis_index("row") * N + H
        column = positions_ref[0, 0, 1, slot] - lax.axis_index("col") * N + H
        turn = jnp.where(column < H, column + H, column - H)
        masks.append((lane >= turn) != (column < H))
        rows.append(row)
        wraps.append(column < H)
        turns.append(turn)

    def align(slot):
        odd = lax.rem(rows[slot], 8)
        return pl.multiple_of(rows[slot] - odd, 8), odd

    def cut(k, slot):
        back = jnp.where(turns[slot] == 0, 0, N - turns[slot])
        start, odd = align(slot)
        first = pltpu.roll(ext[k, pl.ds(start, N + 8), :N], back, 1)
        second = pltpu.roll(ext[k, pl.ds(start, N + 8), N:], back, 1)
        inside = (lane < N - turns[slot]) != wraps[slot]
        value = jnp.where(inside, first, second).reshape(N // 8 + 1, 8, N)
        value = pltpu.roll(value, jnp.where(odd == 0, 0, 8 - odd), 1)
        return jnp.where(sub < 8 - odd, value[:-1], value[1:]).reshape(N, N)

    def both(j):
        re = jnp.concatenate([cut(j, 0), cut(j, 1)], axis=0)
        im = jnp.concatenate([cut(2 + j, 0), cut(2 + j, 1)], axis=0)
        return re, im

    def twice(value):
        return jnp.concatenate([value, value], axis=0)

    f_high, f_low, b_high, b_low = (table_ref[i] for i in range(4))

    def join(re, im):
        return jnp.concatenate([re, im], axis=1)

    def forward(re, im):
        half = from_right(join(re, im), f_high, f_low)
        out = from_left(b_high, b_low, regroup(half))
        return out[:N], out[N:]

    def backward(re, im):
        half = from_left(f_high, f_low, jnp.concatenate([re, im], axis=0))
        out = from_right(regroup(half), b_high, b_low)
        return out[:, :N], out[:, N:]

    probe_re, probe_im = twice(probe_ref[0]), twice(probe_ref[1])
    k_re = jnp.concatenate([kernel_ref[0], kernel_ref[0]], axis=1)
    k_im = jnp.concatenate([kernel_ref[1], kernel_ref[1]], axis=1)
    t_re, t_im = both(0)
    w_re = t_re * probe_re - t_im * probe_im
    w_im = t_re * probe_im + t_im * probe_re
    s_re, s_im = forward(w_re, w_im)
    s_re, s_im = k_re * s_re - k_im * s_im, k_re * s_im + k_im * s_re
    p_re, p_im = backward(s_re, s_im)
    t_re, t_im = both(1)
    w_re = t_re * p_re - t_im * p_im
    w_im = t_re * p_im + t_im * p_re
    far_re, far_im = forward(w_re, w_im)
    target = jnp.concatenate([measured_ref[0], measured_ref[1]], axis=1)
    misfit = far_re * far_re + far_im * far_im - target
    g_re, g_im = backward(misfit * far_re, misfit * far_im)

    def add(k, value):
        for slot in range(2):
            turned = pltpu.roll(value[slot * N : (slot + 1) * N], turns[slot], 1)
            turned = jnp.where(slot < live, turned, 0.0)
            start, odd = align(slot)
            turned = pltpu.roll(turned.reshape(N // 8, 8, N), odd, 1)
            none = jnp.zeros((1, 8, N), F32)
            turned = jnp.concatenate(
                [
                    jnp.where(sub[:1] < odd, none, turned[:1]),
                    jnp.where(sub[1:] < odd, turned[:-1], turned[1:]),
                    jnp.where(sub[:1] < odd, turned[-1:], none),
                ],
                axis=0,
            ).reshape(N + 8, N)
            where = pl.ds(start, N + 8)
            acc[k, where, :N] += jnp.where(masks[slot], turned, 0.0)
            acc[k, where, N:] += jnp.where(masks[slot], 0.0, turned)

    acc[...] = jnp.zeros_like(acc)
    add(1, p_re * g_re + p_im * g_im)
    add(3, p_re * g_im - p_im * g_re)
    g_re, g_im = t_re * g_re + t_im * g_im, t_re * g_im - t_im * g_re
    s_re, s_im = forward(g_re, g_im)
    s_re, s_im = k_re * s_re + k_im * s_im, k_re * s_im - k_im * s_re
    g_re, g_im = backward(s_re, s_im)
    add(0, probe_re * g_re + probe_im * g_im)
    add(2, probe_re * g_im - probe_im * g_re)
    for i in range(2):
        for j in range(2):
            k = 2 * i + j
            mid_ref[i, j] = acc[k, H : 3 * H, :]
            to_even_ref[i, j] = acc[k, strip(3), :]
            to_odd_ref[i, j] = acc[k, strip(0), :]


def fold_rows_kernel(mid_ref, row_even_ref, row_odd_ref, own_ref, even_ref, odd_ref):
    parity = parity_of("col")
    row_parity = parity_of("row")
    for i in range(2):
        for j in range(2):
            even, odd = row_even_ref[1 - row_parity, i, j], row_odd_ref[i, j]
            top = mid_ref[i, j, :H, :] + jnp.where(row_parity == 0, odd, even)
            bottom = mid_ref[i, j, H:, :] + jnp.where(row_parity == 0, even, odd)
            own_ref[i, j, :H, :] = top[:, :N]
            own_ref[i, j, H:, :] = bottom[:, :N]
            odd_ref[i, j], even_ref[i, j] = pack_columns(top[:, N:], bottom[:, N:], parity)


def fold_columns_kernel(own_ref, even_ref, odd_ref, out_ref):
    parity = parity_of("col")
    for i in range(2):
        for j in range(2):
            top, bottom = unpack_columns(odd_ref[i, j], even_ref[1 - parity, i, j], parity)
            out_ref[i, j, :H, :] = own_ref[i, j, :H, :] + top
            out_ref[i, j, H:, :] = own_ref[i, j, H:, :] + bottom


def call(body, shapes, *operands, specs=None, scratch=(), name=None, flops=0):
    outs = [jax.ShapeDtypeStruct(shape, F32) for shape in shapes]
    size = 4 * sum(math.prod(s) for s in shapes) + sum(4 * o.size for o in operands)
    return pl.pallas_call(
        body,
        out_shape=outs,
        in_specs=specs or [VMEM] * len(operands),
        out_specs=[VMEM] * len(outs),
        scratch_shapes=list(scratch),
        compiler_params=pltpu.CompilerParams(vmem_limit_bytes=32 * 2**20),
        cost_estimate=pl.CostEstimate(flops=flops, bytes_accessed=size, transcendentals=0),
        name=name,
    )(*operands)


def exchange(even, odd, axis):
    count = lax.axis_size(axis)
    pairs = [(i, i + 1) for i in range(1, count - 1, 2)]
    odd = lax.ppermute(odd, axis, pairs + [(b, a) for a, b in pairs])
    groups = [[i, i + 1] for i in range(0, count, 2)]
    even = lax.all_gather(even, axis, axis_index_groups=groups)
    return even, odd


def per_device(obj_slices, probe_wave, prop_phase, measured, positions, counts):
    packed = (2, 2, H, N)
    strip = (2, 2, H, 2 * N)
    tile = (2, 2, N, N)
    kernel = jnp.stack([jnp.cos(prop_phase), jnp.sin(prop_phase)])
    tables = jnp.asarray(dft_tables())

    strips = call(pack_kernel, [packed] * 2, obj_slices, name="pack_columns")
    strips = exchange(*strips, "col")
    own = call(rows_kernel, [strip] * 2, obj_slices, *strips, name="pack_rows")
    strips = exchange(*own, "row")
    mid, *strips = call(
        main_kernel,
        [(2, 2, N, 2 * N), strip, strip],
        positions,
        counts,
        *own,
        *strips,
        probe_wave,
        kernel,
        measured[0, 0],
        tables,
        specs=[SMEM] * 2 + [VMEM] * 8,
        scratch=[pltpu.VMEM((4, 2 * N, 2 * N), F32), pltpu.VMEM((4, 2 * N, 2 * N), F32)],
        name="window_gradients",
        flops=36 * 2 * 256**3,
    )
    strips = exchange(*strips, "row")
    own, *strips = call(
        fold_rows_kernel, [tile, packed, packed], mid, *strips, name="fold_rows"
    )
    strips = exchange(*strips, "col")
    (out,) = call(fold_columns_kernel, [tile], own, *strips, name="fold_columns")
    return out


def solution(mesh):
    placed = (
        P(None, None, "row", "col"),
        P(),
        P(),
        P("row", "col", None, None, None),
        P("row", "col", None, None),
        P("row", "col"),
    )
    return jax.shard_map(
        per_device,
        mesh=mesh,
        in_specs=placed,
        out_specs=P(None, None, "row", "col"),
        check_vma=False,
    )
```

```python
import math

import jax
import jax.numpy as jnp
import numpy as np
from jax import lax
from jax.experimental import pallas as pl
from jax.experimental.pallas import tpu as pltpu
from jax.sharding import PartitionSpec as P

N = 128
H = N // 2
F32 = jnp.float32
BF16 = jnp.bfloat16
VMEM = pl.BlockSpec(memory_space=pltpu.VMEM)


def dft_tables():
    index = np.arange(N)
    angle = (index[:, None] * index[None, :] % N) * (-2.0 * math.pi / N)
    re, im = np.cos(angle) / math.sqrt(N), np.sin(angle) / math.sqrt(N)
    table = np.block([[re, im], [-im, re]]).astype(np.float32)
    out = []
    for one in (table, table.T):
        high = one.astype(jnp.bfloat16)
        out += [high, (one - high.astype(np.float32)).astype(jnp.bfloat16)]
    return np.stack(out)


def swap_half(value):
    return pltpu.roll(value, H, value.ndim - 1)


def low_lanes(shape):
    return lax.broadcasted_iota(jnp.int32, shape, len(shape) - 1) < H


def parity_of(axis):
    return lax.rem(lax.axis_index(axis), 2)


def pack_columns(top, bottom, parity):
    bottom = swap_half(bottom)
    low = low_lanes((H, N)) != (parity == 1)
    return jnp.where(low, bottom, top), jnp.where(low, top, bottom)


def unpack_columns(even, odd, parity):
    low = low_lanes((H, N)) != (parity == 1)
    return jnp.where(low, even, odd), swap_half(jnp.where(low, odd, even))


def pack_kernel(obj_ref, even_ref, odd_ref):
    parity = parity_of("col")
    for i in range(2):
        for j in range(2):
            even_ref[i, j], odd_ref[i, j] = pack_columns(
                obj_ref[i, j, :H, :], obj_ref[i, j, H:, :], parity
            )


def rows_kernel(obj_ref, even_ref, odd_ref, row_even_ref, row_odd_ref):
    parity = parity_of("col")
    row_parity = parity_of("row")
    for i in range(2):
        for j in range(2):
            top, bottom = unpack_columns(even_ref[1 - parity, i, j], odd_ref[i, j], parity)
            top = jnp.concatenate([obj_ref[i, j, :H, :], top], axis=1)
            bottom = jnp.concatenate([obj_ref[i, j, H:, :], bottom], axis=1)
            row_even_ref[i, j] = jnp.where(row_parity == 0, bottom, top)
            row_odd_ref[i, j] = jnp.where(row_parity == 0, top, bottom)


def split(value):
    high = value.astype(BF16)
    return high, (value - high.astype(F32)).astype(BF16)


def dot(a, b):
    return jnp.dot(a, b, preferred_element_type=F32)


def from_right(value, high, low):
    v_high, v_low = split(value)
    out = []
    for slot in (slice(0, N), slice(N, 2 * N)):
        both = dot(jnp.concatenate([v_high[slot], v_low[slot]], axis=0), high)
        out.append(both[:N] + (both[N:] + dot(v_high[slot], low)))
    return jnp.concatenate(out, axis=0)


def from_left(high, low, value):
    v_high, v_low = split(value)
    out = []
    for slot in (slice(0, N), slice(N, 2 * N)):
        both = dot(high, jnp.concatenate([v_high[:, slot], v_low[:, slot]], axis=1))
        out.append(both[:, :N] + (both[:, N:] + dot(low, v_high[:, slot])))
    return jnp.concatenate(out, axis=1)


def regroup(value):
    return jnp.concatenate(
        [
            jnp.concatenate([value[:N, :N], value[N:, :N]], axis=1),
            jnp.concatenate([value[:N, N:], value[N:, N:]], axis=1),
        ],
        axis=0,
    )


def strip_rows(number):
    number = jnp.where(parity_of("row") == 0, number, 3 - number)
    return pl.ds(pl.multiple_of(number * H, H), H)


def prepare_kernel(phase_ref, positions_ref, counts_ref, kernel_re_ref, kernel_im_ref, scal_ref):
    kernel_re_ref[...] = jnp.cos(phase_ref[...])
    kernel_im_ref[...] = jnp.sin(phase_ref[...])
    for k, axis in enumerate(("row", "col")):
        first = lax.axis_index(axis) * N - H
        for slot in range(2):
            value = positions_ref[0, 0, k : k + 1, slot : slot + 1] - first
            scal_ref[2 * k + slot : 2 * k + slot + 1, :] = jnp.broadcast_to(value, (1, N))
    scal_ref[4:5, :] = jnp.broadcast_to(counts_ref[...], (1, N))


def main_kernel(
    scal_ref,
    own_even_ref,
    own_odd_ref,
    even_ref,
    odd_ref,
    probe_ref,
    kernel_re_ref,
    kernel_im_ref,
    measured_ref,
    table_ref,
    mid_ref,
    to_even_ref,
    to_odd_ref,
    ext,
    acc,
):
    row_parity = parity_of("row")
    for i in range(2):
        for j in range(2):
            k = 2 * i + j
            ext[k, strip_rows(0), :] = odd_ref[i, j]
            ext[k, strip_rows(1), :] = own_odd_ref[i, j]
            ext[k, strip_rows(2), :] = own_even_ref[i, j]
            ext[k, strip_rows(3), :] = even_ref[1 - row_parity, i, j]
    lane = lax.broadcasted_iota(jnp.int32, (N + 8, N), 1)
    live = jnp.max(scal_ref[4:5, :])
    sub = lax.broadcasted_iota(jnp.int32, (N // 8, 8, N), 1)
    rows, turns, masks, wraps = [], [], [], []
    for slot in range(2):
        row = jnp.max(scal_ref[slot : slot + 1, :])
        column = jnp.max(scal_ref[2 + slot : 3 + slot, :])
        turn = jnp.where(column < H, column + H, column - H)
        masks.append((lane >= turn) != (column < H))
        rows.append(row)
        wraps.append(column < H)
        turns.append(turn)

    def align(slot):
        odd = lax.rem(rows[slot], 8)
        return pl.multiple_of(rows[slot] - odd, 8), odd

    def cut(k, slot):
        back = jnp.where(turns[slot] == 0, 0, N - turns[slot])
        start, odd = align(slot)
        first = pltpu.roll(ext[k, pl.ds(start, N + 8), :N], back, 1)
        second = pltpu.roll(ext[k, pl.ds(start, N + 8), N:], back, 1)
        inside = (lane < N - turns[slot]) != wraps[slot]
        value = jnp.where(inside, first, second).reshape(N // 8 + 1, 8, N)
        value = pltpu.roll(value, jnp.where(odd == 0, 0, 8 - odd), 1)
        return jnp.where(sub < 8 - odd, value[:-1], value[1:]).reshape(N, N)

    def both(j):
        re = jnp.concatenate([cut(j, 0), cut(j, 1)], axis=0)
        im = jnp.concatenate([cut(2 + j, 0), cut(2 + j, 1)], axis=0)
        return re, im

    def twice(value):
        return jnp.concatenate([value, value], axis=0)

    f_high, f_low, b_high, b_low = (table_ref[i] for i in range(4))

    def join(re, im):
        return jnp.concatenate([re, im], axis=1)

    def forward(re, im):
        half = from_right(join(re, im), f_high, f_low)
        out = from_left(b_high, b_low, regroup(half))
        return out[:N], out[N:]

    def backward(re, im):
        half = from_left(f_high, f_low, jnp.concatenate([re, im], axis=0))
        out = from_right(regroup(half), b_high, b_low)
        return out[:, :N], out[:, N:]

    probe_re, probe_im = twice(probe_ref[0]), twice(probe_ref[1])
    k_re = jnp.concatenate([kernel_re_ref[...]] * 2, axis=1)
    k_im = jnp.concatenate([kernel_im_ref[...]] * 2, axis=1)
    t_re, t_im = both(0)
    w_re = t_re * probe_re - t_im * probe_im
    w_im = t_re * probe_im + t_im * probe_re
    s_re, s_im = forward(w_re, w_im)
    s_re, s_im = k_re * s_re - k_im * s_im, k_re * s_im + k_im * s_re
    p_re, p_im = backward(s_re, s_im)
    t_re, t_im = both(1)
    w_re = t_re * p_re - t_im * p_im
    w_im = t_re * p_im + t_im * p_re
    far_re, far_im = forward(w_re, w_im)
    target = jnp.concatenate([measured_ref[0], measured_ref[1]], axis=1)
    misfit = far_re * far_re + far_im * far_im - target
    g_re, g_im = backward(misfit * far_re, misfit * far_im)

    def add(k, value):
        for slot in range(2):
            turned = pltpu.roll(value[slot * N : (slot + 1) * N], turns[slot], 1)
            turned = jnp.where(slot < live, turned, 0.0)
            start, odd = align(slot)
            turned = pltpu.roll(turned.reshape(N // 8, 8, N), odd, 1)
            none = jnp.zeros((1, 8, N), F32)
            turned = jnp.concatenate(
                [
                    jnp.where(sub[:1] < odd, none, turned[:1]),
                    jnp.where(sub[1:] < odd, turned[:-1], turned[1:]),
                    jnp.where(sub[:1] < odd, turned[-1:], none),
                ],
                axis=0,
            ).reshape(N + 8, N)
            where = pl.ds(start, N + 8)
            acc[k, where, :N] += jnp.where(masks[slot], turned, 0.0)
            acc[k, where, N:] += jnp.where(masks[slot], 0.0, turned)

    acc[...] = jnp.zeros_like(acc)
    add(1, p_re * g_re + p_im * g_im)
    add(3, p_re * g_im - p_im * g_re)
    g_re, g_im = t_re * g_re + t_im * g_im, t_re * g_im - t_im * g_re
    s_re, s_im = forward(g_re, g_im)
    s_re, s_im = k_re * s_re + k_im * s_im, k_re * s_im - k_im * s_re
    g_re, g_im = backward(s_re, s_im)
    add(0, probe_re * g_re + probe_im * g_im)
    add(2, probe_re * g_im - probe_im * g_re)
    for i in range(2):
        for j in range(2):
            k = 2 * i + j
            mid_ref[i, j] = acc[k, H : 3 * H, :]
            to_even_ref[i, j] = acc[k, strip_rows(3), :]
            to_odd_ref[i, j] = acc[k, strip_rows(0), :]


def fold_rows_kernel(mid_ref, row_even_ref, row_odd_ref, own_ref, even_ref, odd_ref):
    parity = parity_of("col")
    row_parity = parity_of("row")
    for i in range(2):
        for j in range(2):
            even, odd = row_even_ref[1 - row_parity, i, j], row_odd_ref[i, j]
            top = mid_ref[i, j, :H, :] + jnp.where(row_parity == 0, odd, even)
            bottom = mid_ref[i, j, H:, :] + jnp.where(row_parity == 0, even, odd)
            own_ref[i, j, :H, :] = top[:, :N]
            own_ref[i, j, H:, :] = bottom[:, :N]
            odd_ref[i, j], even_ref[i, j] = pack_columns(top[:, N:], bottom[:, N:], parity)


def fold_columns_kernel(own_ref, even_ref, odd_ref, out_ref):
    parity = parity_of("col")
    for i in range(2):
        for j in range(2):
            top, bottom = unpack_columns(odd_ref[i, j], even_ref[1 - parity, i, j], parity)
            out_ref[i, j, :H, :] = own_ref[i, j, :H, :] + top
            out_ref[i, j, H:, :] = own_ref[i, j, H:, :] + bottom


def call(body, shapes, *operands, kinds=None, scratch=(), name=None, flops=0):
    kinds = kinds or [F32] * len(shapes)
    size = 4 * sum(math.prod(s) for s in shapes) + sum(4 * o.size for o in operands)
    return pl.pallas_call(
        body,
        out_shape=[jax.ShapeDtypeStruct(*each) for each in zip(shapes, kinds)],
        in_specs=[VMEM] * len(operands),
        out_specs=[VMEM] * len(shapes),
        scratch_shapes=list(scratch),
        compiler_params=pltpu.CompilerParams(vmem_limit_bytes=32 * 2**20),
        cost_estimate=pl.CostEstimate(flops=flops, bytes_accessed=size, transcendentals=0),
        name=name,
    )(*operands)


def exchange(even, odd, axis):
    count = lax.axis_size(axis)
    pairs = [(i, i + 1) for i in range(1, count - 1, 2)]
    odd = lax.ppermute(odd, axis, pairs + [(b, a) for a, b in pairs])
    groups = [[i, i + 1] for i in range(0, count, 2)]
    even = lax.all_gather(even, axis, axis_index_groups=groups)
    return even, odd


def per_device(obj_slices, probe_wave, prop_phase, measured, positions, counts):
    packed = (2, 2, H, N)
    strip = (2, 2, H, 2 * N)
    tile = (2, 2, N, N)
    tables = jnp.asarray(dft_tables())

    strips = call(pack_kernel, [packed] * 2, obj_slices, name="pack_columns")
    strips = exchange(*strips, "col")
    own = call(rows_kernel, [strip] * 2, obj_slices, *strips, name="pack_rows")
    even, odd = exchange(*own, "row")
    even, *rest = lax.optimization_barrier((even, prop_phase, positions, counts))
    kernel_re, kernel_im, scalars = call(
        prepare_kernel, [(N, N), (N, N), (8, N)], *rest, kinds=[F32, F32, jnp.int32], name="prepare"
    )
    mid, *strips = call(
        main_kernel,
        [(2, 2, N, 2 * N), strip, strip],
        scalars,
        *own,
        even,
        odd,
        probe_wave,
        kernel_re,
        kernel_im,
        measured[0, 0],
        tables,
        scratch=[pltpu.VMEM((4, 2 * N, 2 * N), F32), pltpu.VMEM((4, 2 * N, 2 * N), F32)],
        name="window_gradients",
        flops=36 * 2 * 256**3,
    )
    strips = exchange(*strips, "row")
    own, *strips = call(
        fold_rows_kernel, [tile, packed, packed], mid, *strips, name="fold_rows"
    )
    strips = exchange(*strips, "col")
    (out,) = call(fold_columns_kernel, [tile], own, *strips, name="fold_columns")
    return out


def solution(mesh):
    placed = (
        P(None, None, "row", "col"),
        P(),
        P(),
        P("row", "col", None, None, None),
        P("row", "col", None, None),
        P("row", "col"),
    )
    return jax.shard_map(
        per_device,
        mesh=mesh,
        in_specs=placed,
        out_specs=P(None, None, "row", "col"),
        check_vma=False,
    )
```

```python
import math

import jax
import jax.numpy as jnp
import numpy as np
from jax import lax
from jax.experimental import pallas as pl
from jax.experimental.pallas import tpu as pltpu
from jax.sharding import PartitionSpec as P

N = 128
H = N // 2
F32 = jnp.float32
BF16 = jnp.bfloat16
VMEM = pl.BlockSpec(memory_space=pltpu.VMEM)


def dft_tables():
    index = np.arange(N)
    angle = (index[:, None] * index[None, :] % N) * (-2.0 * math.pi / N)
    re, im = np.cos(angle) / math.sqrt(N), np.sin(angle) / math.sqrt(N)
    table = np.block([[re, im], [-im, re]]).astype(np.float32)
    out = []
    for one in (table, table.T):
        high = one.astype(jnp.bfloat16)
        out += [high, (one - high.astype(np.float32)).astype(jnp.bfloat16)]
    return np.stack(out)


def swap_half(value):
    return pltpu.roll(value, H, value.ndim - 1)


def low_lanes(shape):
    return lax.broadcasted_iota(jnp.int32, shape, len(shape) - 1) < H


def parity_of(axis):
    return lax.rem(lax.axis_index(axis), 2)


def pack_columns(top, bottom, parity):
    bottom = swap_half(bottom)
    low = low_lanes((H, N)) != (parity == 1)
    return jnp.where(low, bottom, top), jnp.where(low, top, bottom)


def unpack_columns(even, odd, parity):
    low = low_lanes((H, N)) != (parity == 1)
    return jnp.where(low, even, odd), swap_half(jnp.where(low, odd, even))


def pack_kernel(obj_ref, even_ref, odd_ref):
    parity = parity_of("col")
    for i in range(2):
        for j in range(2):
            even_ref[i, j], odd_ref[i, j] = pack_columns(
                obj_ref[i, j, :H, :], obj_ref[i, j, H:, :], parity
            )


def rows_kernel(obj_ref, even_ref, odd_ref, row_even_ref, row_odd_ref):
    parity = parity_of("col")
    row_parity = parity_of("row")
    for i in range(2):
        for j in range(2):
            top, bottom = unpack_columns(even_ref[1 - parity, i, j], odd_ref[i, j], parity)
            top = jnp.concatenate([obj_ref[i, j, :H, :], top], axis=1)
            bottom = jnp.concatenate([obj_ref[i, j, H:, :], bottom], axis=1)
            row_even_ref[i, j] = jnp.where(row_parity == 0, bottom, top)
            row_odd_ref[i, j] = jnp.where(row_parity == 0, top, bottom)


def split(value):
    high = value.astype(BF16)
    return high, (value - high.astype(F32)).astype(BF16)


def dot(a, b):
    return jnp.dot(a, b, preferred_element_type=F32)


def from_right(value, high, low):
    v_high, v_low = split(value)
    out = []
    for q in range(4):
        slot = slice(q * H, (q + 1) * H)
        both = dot(jnp.concatenate([v_high[slot], v_low[slot]], axis=0), high)
        out.append(both[:H] + (both[H:] + dot(v_high[slot], low)))
    return jnp.concatenate(out, axis=0)


def from_left(high, low, value):
    v_high, v_low = split(value)
    out = []
    for slot in (slice(0, N), slice(N, 2 * N)):
        both = dot(high, jnp.concatenate([v_high[:, slot], v_low[:, slot]], axis=1))
        out.append(both[:, :N] + (both[:, N:] + dot(low, v_high[:, slot])))
    return jnp.concatenate(out, axis=1)


def regroup(value):
    return jnp.concatenate(
        [
            jnp.concatenate([value[:N, :N], value[N:, :N]], axis=1),
            jnp.concatenate([value[:N, N:], value[N:, N:]], axis=1),
        ],
        axis=0,
    )


def strip_rows(number):
    number = jnp.where(parity_of("row") == 0, number, 3 - number)
    return pl.ds(pl.multiple_of(number * H, H), H)


def prepare_kernel(phase_ref, positions_ref, counts_ref, kernel_re_ref, kernel_im_ref, scal_ref):
    kernel_re_ref[...] = jnp.cos(phase_ref[...])
    kernel_im_ref[...] = jnp.sin(phase_ref[...])
    for k, axis in enumerate(("row", "col")):
        first = lax.axis_index(axis) * N - H
        for slot in range(2):
            value = positions_ref[0, 0, k : k + 1, slot : slot + 1] - first
            scal_ref[2 * k + slot : 2 * k + slot + 1, :] = jnp.broadcast_to(value, (1, N))
    scal_ref[4:5, :] = jnp.broadcast_to(counts_ref[...], (1, N))


def main_kernel(
    scal_ref,
    own_even_ref,
    own_odd_ref,
    even_ref,
    odd_ref,
    probe_ref,
    kernel_re_ref,
    kernel_im_ref,
    measured_ref,
    table_ref,
    mid_ref,
    to_even_ref,
    to_odd_ref,
    ext,
    acc,
):
    row_parity = parity_of("row")
    for i in range(2):
        for j in range(2):
            k = 2 * i + j
            ext[k, strip_rows(0), :] = odd_ref[i, j]
            ext[k, strip_rows(1), :] = own_odd_ref[i, j]
            ext[k, strip_rows(2), :] = own_even_ref[i, j]
            ext[k, strip_rows(3), :] = even_ref[1 - row_parity, i, j]
    lane = lax.broadcasted_iota(jnp.int32, (N + 8, N), 1)
    live = jnp.max(scal_ref[4:5, :])
    sub = lax.broadcasted_iota(jnp.int32, (N // 8, 8, N), 1)
    rows, turns, masks, wraps = [], [], [], []
    for slot in range(2):
        row = jnp.max(scal_ref[slot : slot + 1, :])
        column = jnp.max(scal_ref[2 + slot : 3 + slot, :])
        turn = jnp.where(column < H, column + H, column - H)
        masks.append((lane >= turn) != (column < H))
        rows.append(row)
        wraps.append(column < H)
        turns.append(turn)

    def align(slot):
        odd = lax.rem(rows[slot], 8)
        return pl.multiple_of(rows[slot] - odd, 8), odd

    def cut(k, slot):
        back = jnp.where(turns[slot] == 0, 0, N - turns[slot])
        start, odd = align(slot)
        first = pltpu.roll(ext[k, pl.ds(start, N + 8), :N], back, 1)
        second = pltpu.roll(ext[k, pl.ds(start, N + 8), N:], back, 1)
        inside = (lane < N - turns[slot]) != wraps[slot]
        value = jnp.where(inside, first, second).reshape(N // 8 + 1, 8, N)
        value = pltpu.roll(value, jnp.where(odd == 0, 0, 8 - odd), 1)
        return jnp.where(sub < 8 - odd, value[:-1], value[1:]).reshape(N, N)

    def both(j):
        re = jnp.concatenate([cut(j, 0), cut(j, 1)], axis=0)
        im = jnp.concatenate([cut(2 + j, 0), cut(2 + j, 1)], axis=0)
        return re, im

    def twice(value):
        return jnp.concatenate([value, value], axis=0)

    f_high, f_low, b_high, b_low = (table_ref[i] for i in range(4))

    def join(re, im):
        return jnp.concatenate([re, im], axis=1)

    def forward(re, im):
        half = from_right(join(re, im), f_high, f_low)
        out = from_left(b_high, b_low, regroup(half))
        return out[:N], out[N:]

    def backward(re, im):
        half = from_left(f_high, f_low, jnp.concatenate([re, im], axis=0))
        out = from_right(regroup(half), b_high, b_low)
        return out[:, :N], out[:, N:]

    probe_re, probe_im = twice(probe_ref[0]), twice(probe_ref[1])
    k_re = jnp.concatenate([kernel_re_ref[...]] * 2, axis=1)
    k_im = jnp.concatenate([kernel_im_ref[...]] * 2, axis=1)
    t_re, t_im = both(0)
    w_re = t_re * probe_re - t_im * probe_im
    w_im = t_re * probe_im + t_im * probe_re
    s_re, s_im = forward(w_re, w_im)
    s_re, s_im = k_re * s_re - k_im * s_im, k_re * s_im + k_im * s_re
    p_re, p_im = backward(s_re, s_im)
    t_re, t_im = both(1)
    w_re = t_re * p_re - t_im * p_im
    w_im = t_re * p_im + t_im * p_re
    far_re, far_im = forward(w_re, w_im)
    target = jnp.concatenate([measured_ref[0], measured_ref[1]], axis=1)
    misfit = far_re * far_re + far_im * far_im - target
    g_re, g_im = backward(misfit * far_re, misfit * far_im)

    def add(k, value):
        for slot in range(2):
            turned = pltpu.roll(value[slot * N : (slot + 1) * N], turns[slot], 1)
            turned = jnp.where(slot < live, turned, 0.0)
            start, odd = align(slot)
            turned = pltpu.roll(turned.reshape(N // 8, 8, N), odd, 1)
            none = jnp.zeros((1, 8, N), F32)
            turned = jnp.concatenate(
                [
                    jnp.where(sub[:1] < odd, none, turned[:1]),
                    jnp.where(sub[1:] < odd, turned[:-1], turned[1:]),
                    jnp.where(sub[:1] < odd, turned[-1:], none),
                ],
                axis=0,
            ).reshape(N + 8, N)
            where = pl.ds(start, N + 8)
            acc[k, where, :N] += jnp.where(masks[slot], turned, 0.0)
            acc[k, where, N:] += jnp.where(masks[slot], 0.0, turned)

    acc[...] = jnp.zeros_like(acc)
    add(1, p_re * g_re + p_im * g_im)
    add(3, p_re * g_im - p_im * g_re)
    g_re, g_im = t_re * g_re + t_im * g_im, t_re * g_im - t_im * g_re
    s_re, s_im = forward(g_re, g_im)
    s_re, s_im = k_re * s_re + k_im * s_im, k_re * s_im - k_im * s_re
    g_re, g_im = backward(s_re, s_im)
    add(0, probe_re * g_re + probe_im * g_im)
    add(2, probe_re * g_im - probe_im * g_re)
    for i in range(2):
        for j in range(2):
            k = 2 * i + j
            mid_ref[i, j] = acc[k, H : 3 * H, :]
            to_even_ref[i, j] = acc[k, strip_rows(3), :]
            to_odd_ref[i, j] = acc[k, strip_rows(0), :]


def fold_rows_kernel(mid_ref, row_even_ref, row_odd_ref, own_ref, even_ref, odd_ref):
    parity = parity_of("col")
    row_parity = parity_of("row")
    for i in range(2):
        for j in range(2):
            even, odd = row_even_ref[1 - row_parity, i, j], row_odd_ref[i, j]
            top = mid_ref[i, j, :H, :] + jnp.where(row_parity == 0, odd, even)
            bottom = mid_ref[i, j, H:, :] + jnp.where(row_parity == 0, even, odd)
            own_ref[i, j, :H, :] = top[:, :N]
            own_ref[i, j, H:, :] = bottom[:, :N]
            odd_ref[i, j], even_ref[i, j] = pack_columns(top[:, N:], bottom[:, N:], parity)


def fold_columns_kernel(own_ref, even_ref, odd_ref, out_ref):
    parity = parity_of("col")
    for i in range(2):
        for j in range(2):
            top, bottom = unpack_columns(odd_ref[i, j], even_ref[1 - parity, i, j], parity)
            out_ref[i, j, :H, :] = own_ref[i, j, :H, :] + top
            out_ref[i, j, H:, :] = own_ref[i, j, H:, :] + bottom


def call(body, shapes, *operands, kinds=None, scratch=(), name=None, flops=0):
    kinds = kinds or [F32] * len(shapes)
    size = 4 * sum(math.prod(s) for s in shapes) + sum(4 * o.size for o in operands)
    return pl.pallas_call(
        body,
        out_shape=[jax.ShapeDtypeStruct(*each) for each in zip(shapes, kinds)],
        in_specs=[VMEM] * len(operands),
        out_specs=[VMEM] * len(shapes),
        scratch_shapes=list(scratch),
        compiler_params=pltpu.CompilerParams(vmem_limit_bytes=32 * 2**20),
        cost_estimate=pl.CostEstimate(flops=flops, bytes_accessed=size, transcendentals=0),
        name=name,
    )(*operands)


def exchange(even, odd, axis):
    count = lax.axis_size(axis)
    pairs = [(i, i + 1) for i in range(1, count - 1, 2)]
    odd = lax.ppermute(odd, axis, pairs + [(b, a) for a, b in pairs])
    groups = [[i, i + 1] for i in range(0, count, 2)]
    even = lax.all_gather(even, axis, axis_index_groups=groups)
    return even, odd


def per_device(obj_slices, probe_wave, prop_phase, measured, positions, counts):
    packed = (2, 2, H, N)
    strip = (2, 2, H, 2 * N)
    tile = (2, 2, N, N)
    tables = jnp.asarray(dft_tables())

    strips = call(pack_kernel, [packed] * 2, obj_slices, name="pack_columns")
    strips = exchange(*strips, "col")
    own = call(rows_kernel, [strip] * 2, obj_slices, *strips, name="pack_rows")
    even, odd = exchange(*own, "row")
    even, *rest = lax.optimization_barrier((even, prop_phase, positions, counts))
    kernel_re, kernel_im, scalars = call(
        prepare_kernel, [(N, N), (N, N), (8, N)], *rest, kinds=[F32, F32, jnp.int32], name="prepare"
    )
    mid, *strips = call(
        main_kernel,
        [(2, 2, N, 2 * N), strip, strip],
        scalars,
        *own,
        even,
        odd,
        probe_wave,
        kernel_re,
        kernel_im,
        measured[0, 0],
        tables,
        scratch=[pltpu.VMEM((4, 2 * N, 2 * N), F32), pltpu.VMEM((4, 2 * N, 2 * N), F32)],
        name="window_gradients",
        flops=36 * 2 * 256**3,
    )
    strips = exchange(*strips, "row")
    own, *strips = call(
        fold_rows_kernel, [tile, packed, packed], mid, *strips, name="fold_rows"
    )
    strips = exchange(*strips, "col")
    (out,) = call(fold_columns_kernel, [tile], own, *strips, name="fold_columns")
    return out


def solution(mesh):
    placed = (
        P(None, None, "row", "col"),
        P(),
        P(),
        P("row", "col", None, None, None),
        P("row", "col", None, None),
        P("row", "col"),
    )
    return jax.shard_map(
        per_device,
        mesh=mesh,
        in_specs=placed,
        out_specs=P(None, None, "row", "col"),
        check_vma=False,
    )
```

```python
import math

import jax
import jax.numpy as jnp
import numpy as np
from jax import lax
from jax.experimental import pallas as pl
from jax.experimental.pallas import tpu as pltpu
from jax.sharding import PartitionSpec as P

N = 128
H = N // 2
F32 = jnp.float32
BF16 = jnp.bfloat16
VMEM = pl.BlockSpec(memory_space=pltpu.VMEM)


def dft_tables():
    index = np.arange(N)
    angle = (index[:, None] * index[None, :] % N) * (-2.0 * math.pi / N)
    re, im = np.cos(angle) / math.sqrt(N), np.sin(angle) / math.sqrt(N)
    table = np.block([[re, im], [-im, re]]).astype(np.float32)
    out = []
    for one in (table, table.T):
        high = one.astype(jnp.bfloat16)
        out += [high, (one - high.astype(np.float32)).astype(jnp.bfloat16)]
    return np.stack(out)


def swap_half(value):
    return pltpu.roll(value, H, value.ndim - 1)


def low_lanes(shape):
    return lax.broadcasted_iota(jnp.int32, shape, len(shape) - 1) < H


def parity_of(axis):
    return lax.rem(lax.axis_index(axis), 2)


def pack_columns(top, bottom, parity):
    bottom = swap_half(bottom)
    low = low_lanes((H, N)) != (parity == 1)
    return jnp.where(low, bottom, top), jnp.where(low, top, bottom)


def unpack_columns(even, odd, parity):
    low = low_lanes((H, N)) != (parity == 1)
    return jnp.where(low, even, odd), swap_half(jnp.where(low, odd, even))


def pack_kernel(obj_ref, even_ref, odd_ref):
    parity = parity_of("col")
    for i in range(2):
        for j in range(2):
            even_ref[i, j], odd_ref[i, j] = pack_columns(
                obj_ref[i, j, :H, :], obj_ref[i, j, H:, :], parity
            )


def rows_kernel(obj_ref, even_ref, odd_ref, row_even_ref, row_odd_ref):
    parity = parity_of("col")
    row_parity = parity_of("row")
    for i in range(2):
        for j in range(2):
            top, bottom = unpack_columns(even_ref[1 - parity, i, j], odd_ref[i, j], parity)
            top = jnp.concatenate([obj_ref[i, j, :H, :], top], axis=1)
            bottom = jnp.concatenate([obj_ref[i, j, H:, :], bottom], axis=1)
            row_even_ref[i, j] = jnp.where(row_parity == 0, bottom, top)
            row_odd_ref[i, j] = jnp.where(row_parity == 0, top, bottom)


def split(value):
    high = value.astype(BF16)
    return high, (value - high.astype(F32)).astype(BF16)


def dot(a, b):
    return jnp.dot(a, b, preferred_element_type=F32)


def from_right(value, high, low):
    v_high, v_low = split(value)
    out = []
    for q in range(4):
        slot = slice(q * H, (q + 1) * H)
        both = dot(jnp.concatenate([v_high[slot], v_low[slot]], axis=0), high)
        out.append(both[:H] + (both[H:] + dot(v_high[slot], low)))
    return jnp.concatenate(out, axis=0)


def from_left(high, low, value):
    v_high, v_low = split(value)
    out = []
    for slot in (slice(0, N), slice(N, 2 * N)):
        both = dot(high, jnp.concatenate([v_high[:, slot], v_low[:, slot]], axis=1))
        out.append(both[:, :N] + (both[:, N:] + dot(low, v_high[:, slot])))
    return jnp.concatenate(out, axis=1)


def regroup(value):
    return jnp.concatenate(
        [
            jnp.concatenate([value[:N, :N], value[N:, :N]], axis=1),
            jnp.concatenate([value[:N, N:], value[N:, N:]], axis=1),
        ],
        axis=0,
    )


def strip_rows(number):
    number = jnp.where(parity_of("row") == 0, number, 3 - number)
    return pl.ds(pl.multiple_of(number * H, H), H)


def prepare_kernel(phase_ref, positions_ref, counts_ref, kernel_re_ref, kernel_im_ref, scal_ref):
    kernel_re_ref[...] = jnp.cos(phase_ref[...])
    kernel_im_ref[...] = jnp.sin(phase_ref[...])
    for k, axis in enumerate(("row", "col")):
        first = lax.axis_index(axis) * N - H
        for slot in range(2):
            value = positions_ref[0, 0, k : k + 1, slot : slot + 1] - first
            scal_ref[2 * k + slot : 2 * k + slot + 1, :] = jnp.broadcast_to(value, (1, N))
    scal_ref[4:5, :] = jnp.broadcast_to(counts_ref[...], (1, N))


def main_kernel(
    scal_ref,
    own_even_ref,
    own_odd_ref,
    even_ref,
    odd_ref,
    probe_ref,
    kernel_re_ref,
    kernel_im_ref,
    measured_ref,
    table_ref,
    mid_ref,
    to_even_ref,
    to_odd_ref,
    ext,
    acc,
):
    row_parity = parity_of("row")
    for i in range(2):
        for j in range(2):
            k = 2 * i + j
            ext[k, strip_rows(0), :] = odd_ref[i, j]
            ext[k, strip_rows(1), :] = own_odd_ref[i, j]
            ext[k, strip_rows(2), :] = own_even_ref[i, j]
            ext[k, strip_rows(3), :] = even_ref[1 - row_parity, i, j]
    lane = lax.broadcasted_iota(jnp.int32, (N + 8, N), 1)
    live = jnp.max(scal_ref[4:5, :])
    sub = lax.broadcasted_iota(jnp.int32, (N // 8, 8, N), 1)
    rows, turns, masks, wraps = [], [], [], []
    for slot in range(2):
        row = jnp.max(scal_ref[slot : slot + 1, :])
        column = jnp.max(scal_ref[2 + slot : 3 + slot, :])
        turn = jnp.where(column < H, column + H, column - H)
        masks.append((lane >= turn) != (column < H))
        rows.append(row)
        wraps.append(column < H)
        turns.append(turn)

    def align(slot):
        odd = lax.rem(rows[slot], 8)
        return pl.multiple_of(rows[slot] - odd, 8), odd

    def cut(k, slot):
        back = jnp.where(turns[slot] == 0, 0, N - turns[slot])
        start, odd = align(slot)
        first = pltpu.roll(ext[k, pl.ds(start, N + 8), :N], back, 1)
        second = pltpu.roll(ext[k, pl.ds(start, N + 8), N:], back, 1)
        inside = (lane < N - turns[slot]) != wraps[slot]
        value = jnp.where(inside, first, second).reshape(N // 8 + 1, 8, N)
        value = pltpu.roll(value, jnp.where(odd == 0, 0, 8 - odd), 1)
        return jnp.where(sub < 8 - odd, value[:-1], value[1:]).reshape(N, N)

    def both(j):
        re = jnp.concatenate([cut(j, 0), cut(j, 1)], axis=0)
        im = jnp.concatenate([cut(2 + j, 0), cut(2 + j, 1)], axis=0)
        return re, im

    def twice(value):
        return jnp.concatenate([value, value], axis=0)

    f_high, f_low, b_high, b_low = (table_ref[i] for i in range(4))

    def join(re, im):
        return jnp.concatenate([re, im], axis=1)

    def forward(re, im):
        half = from_right(join(re, im), f_high, f_low)
        out = from_left(b_high, b_low, regroup(half))
        return out[:N], out[N:]

    def backward(re, im):
        half = from_left(f_high, f_low, jnp.concatenate([re, im], axis=0))
        out = from_right(regroup(half), b_high, b_low)
        return out[:, :N], out[:, N:]

    probe_re, probe_im = twice(probe_ref[0]), twice(probe_ref[1])
    k_re = jnp.concatenate([kernel_re_ref[...]] * 2, axis=1)
    k_im = jnp.concatenate([kernel_im_ref[...]] * 2, axis=1)
    t_re, t_im = both(0)
    w_re = t_re * probe_re - t_im * probe_im
    w_im = t_re * probe_im + t_im * probe_re
    s_re, s_im = forward(w_re, w_im)
    s_re, s_im = k_re * s_re - k_im * s_im, k_re * s_im + k_im * s_re
    p_re, p_im = backward(s_re, s_im)
    t_re, t_im = both(1)
    w_re = t_re * p_re - t_im * p_im
    w_im = t_re * p_im + t_im * p_re
    far_re, far_im = forward(w_re, w_im)
    target = jnp.concatenate([measured_ref[0], measured_ref[1]], axis=1)
    misfit = far_re * far_re + far_im * far_im - target
    g_re, g_im = backward(misfit * far_re, misfit * far_im)

    def add(k, value):
        for slot in range(2):
            turned = pltpu.roll(value[slot * N : (slot + 1) * N], turns[slot], 1)
            turned = jnp.where(slot < live, turned, 0.0)
            start, odd = align(slot)
            turned = pltpu.roll(turned.reshape(N // 8, 8, N), odd, 1)
            none = jnp.zeros((1, 8, N), F32)
            turned = jnp.concatenate(
                [
                    jnp.where(sub[:1] < odd, none, turned[:1]),
                    jnp.where(sub[1:] < odd, turned[:-1], turned[1:]),
                    jnp.where(sub[:1] < odd, turned[-1:], none),
                ],
                axis=0,
            ).reshape(N + 8, N)
            where = pl.ds(start, N + 8)
            acc[k, where, :N] += jnp.where(masks[slot], turned, 0.0)
            acc[k, where, N:] += jnp.where(masks[slot], 0.0, turned)

    acc[...] = jnp.zeros_like(acc)
    add(1, p_re * g_re + p_im * g_im)
    add(3, p_re * g_im - p_im * g_re)
    g_re, g_im = t_re * g_re + t_im * g_im, t_re * g_im - t_im * g_re
    s_re, s_im = forward(g_re, g_im)
    s_re, s_im = k_re * s_re + k_im * s_im, k_re * s_im - k_im * s_re
    g_re, g_im = backward(s_re, s_im)
    add(0, probe_re * g_re + probe_im * g_im)
    add(2, probe_re * g_im - probe_im * g_re)
    for i in range(2):
        for j in range(2):
            k = 2 * i + j
            mid_ref[i, j] = acc[k, H : 3 * H, :]
            to_even_ref[i, j] = acc[k, strip_rows(3), :]
            to_odd_ref[i, j] = acc[k, strip_rows(0), :]


def fold_rows_kernel(mid_ref, row_even_ref, row_odd_ref, own_ref, even_ref, odd_ref):
    parity = parity_of("col")
    row_parity = parity_of("row")
    for i in range(2):
        for j in range(2):
            even, odd = row_even_ref[1 - row_parity, i, j], row_odd_ref[i, j]
            top = mid_ref[i, j, :H, :] + jnp.where(row_parity == 0, odd, even)
            bottom = mid_ref[i, j, H:, :] + jnp.where(row_parity == 0, even, odd)
            own_ref[i, j, :H, :] = top[:, :N]
            own_ref[i, j, H:, :] = bottom[:, :N]
            odd_ref[i, j], even_ref[i, j] = pack_columns(top[:, N:], bottom[:, N:], parity)


def fold_columns_kernel(own_ref, even_ref, odd_ref, out_ref):
    parity = parity_of("col")
    for i in range(2):
        for j in range(2):
            top, bottom = unpack_columns(odd_ref[i, j], even_ref[1 - parity, i, j], parity)
            out_ref[i, j, :H, :] = own_ref[i, j, :H, :] + top
            out_ref[i, j, H:, :] = own_ref[i, j, H:, :] + bottom


def call(body, shapes, *operands, kinds=None, scratch=(), name=None, flops=0):
    kinds = kinds or [F32] * len(shapes)
    size = 4 * sum(math.prod(s) for s in shapes) + sum(4 * o.size for o in operands)
    return pl.pallas_call(
        body,
        out_shape=[jax.ShapeDtypeStruct(*each) for each in zip(shapes, kinds)],
        in_specs=[VMEM] * len(operands),
        out_specs=[VMEM] * len(shapes),
        scratch_shapes=list(scratch),
        compiler_params=pltpu.CompilerParams(vmem_limit_bytes=32 * 2**20),
        cost_estimate=pl.CostEstimate(flops=flops, bytes_accessed=size, transcendentals=0),
        name=name,
    )(*operands)


def exchange(even, odd, axis):
    count = lax.axis_size(axis)
    pairs = [(i, i + 1) for i in range(1, count - 1, 2)]
    odd = lax.ppermute(odd, axis, pairs + [(b, a) for a, b in pairs])
    groups = [[i, i + 1] for i in range(0, count, 2)]
    even = lax.all_gather(even, axis, axis_index_groups=groups)
    return even, odd


def per_device(obj_slices, probe_wave, prop_phase, measured, positions, counts):
    packed = (2, 2, H, N)
    strip = (2, 2, H, 2 * N)
    tile = (2, 2, N, N)
    tables = jnp.asarray(dft_tables())

    strips = call(pack_kernel, [packed] * 2, obj_slices, name="pack_columns")
    strips = exchange(*strips, "col")
    own = call(rows_kernel, [strip] * 2, obj_slices, *strips, name="pack_rows")
    even, odd = exchange(*own, "row")
    even, prop_phase = lax.optimization_barrier((even, prop_phase))
    rest = (prop_phase, positions, counts)
    kernel_re, kernel_im, scalars = call(
        prepare_kernel, [(N, N), (N, N), (8, N)], *rest, kinds=[F32, F32, jnp.int32], name="prepare"
    )
    mid, *strips = call(
        main_kernel,
        [(2, 2, N, 2 * N), strip, strip],
        scalars,
        *own,
        even,
        odd,
        probe_wave,
        kernel_re,
        kernel_im,
        measured[0, 0],
        tables,
        scratch=[pltpu.VMEM((4, 2 * N, 2 * N), F32), pltpu.VMEM((4, 2 * N, 2 * N), F32)],
        name="window_gradients",
        flops=36 * 2 * 256**3,
    )
    strips = exchange(*strips, "row")
    own, *strips = call(
        fold_rows_kernel, [tile, packed, packed], mid, *strips, name="fold_rows"
    )
    strips = exchange(*strips, "col")
    (out,) = call(fold_columns_kernel, [tile], own, *strips, name="fold_columns")
    return out


def solution(mesh):
    placed = (
        P(None, None, "row", "col"),
        P(),
        P(),
        P("row", "col", None, None, None),
        P("row", "col", None, None),
        P("row", "col"),
    )
    return jax.shard_map(
        per_device,
        mesh=mesh,
        in_specs=placed,
        out_specs=P(None, None, "row", "col"),
        check_vma=False,
    )
```
